32 devices in a mesh: node: 4 (over z), local: 2 (over x), dp: 4 (over y, core).
Axes of the slice: x: 2, y: 2, z: 4, core: 2. Of those that a mesh axis runs over, the one named last changes fastest.
Arguments:
- layer_input: bfloat16 [2048, 2560], P(('node', 'dp'), 'local'), may hold values from -6 to 6
- grad_out: bfloat16 [2048, 2560], P(('node', 'dp'), 'local'), may hold values from -6 to 6
- gate_values: bfloat16 [2048, 6], P(('node', 'dp')), may hold values from 0.049804688 to 0.5
- route_expert: int32 [2048, 6], P(('node', 'dp')), may hold values from 0 to 39, as said below
- route_slot: int32 [2048, 6], P(('node', 'dp')), may hold values from -1 to 5, as said below
- shared_gate: bfloat16 [1536, 2560], P('local', 'dp'), may hold values from -0.125 to 0.125
- shared_up: bfloat16 [1536, 2560], P('local', 'dp'), may hold values from -0.125 to 0.125
- shared_down: bfloat16 [1536, 2560], P('local', 'dp'), may hold values from -0.15625 to 0.15625
- expert_gate: bfloat16 [16, 768, 2560], P(('node', 'dp'), 'local'), may hold values from -0.125 to 0.125
- expert_up: bfloat16 [16, 768, 2560], P(('node', 'dp'), 'local'), may hold values from -0.125 to 0.125
- expert_down: bfloat16 [16, 768, 2560], P(('node', 'dp'), 'local'), may hold values from -0.21875 to 0.21875
Outputs:
- grad_x: bfloat16 [2048, 2560], P(('node', 'dp'), 'local')
- grad_gates: float32 [2048, 6], P(('node', 'dp'))
- grad_shared_gate: bfloat16 [1536, 2560], P('local', 'dp')
- grad_shared_up: bfloat16 [1536, 2560], P('local', 'dp')
- grad_shared_down: bfloat16 [1536, 2560], P('local', 'dp')
- grad_expert_gate: bfloat16 [16, 768, 2560], P(('node', 'dp'), 'local')
- grad_expert_up: bfloat16 [16, 768, 2560], P(('node', 'dp'), 'local')
- grad_expert_down: bfloat16 [16, 768, 2560], P(('node', 'dp'), 'local')
The draws below stay inside these ranges and needn't reach their ends.
Inputs may be any that keep to these rules, and one draw needn't show every extreme that they name: `route_expert`: each row names 6 different experts, all on at most 3 nodes; expert i lies on node i // 10. `route_slot`: for the choice of expert i, counting the choices of the 128 tokens of one group to the same expert in the order of rows, then of columns, from 0: the slot is that count, and it is -1 exactly where i % 10 >= 4 or the count reaches 6.
All inputs are finite; a program needn't handle non-finite values.
Results may differ from the reference program's by a relative error of at most 0.025.
Values may be sent and summed in bfloat16 or wider, within the bound.
No kernel may reach another device: no remote copies, remote signals or barrier semaphores. Data moves between devices by JAX's collectives and lax.ppermute only.
A program may use at most 128 MiB of HBM per device.

```python
import jax
import jax.numpy as jnp
from jax import lax

D = 2560
FS = 1536
FR = 768
TOK = 128
TOPK = 6
NODE_LIMIT = 3
NODE_EXPERTS = 10
CAP = 6
EXPERTS = 16
TOKENS = 2048
N_NODE = 4
N_LOCAL = 2
N_DP = 4


def routing(key):
    groups = N_NODE * N_DP
    key_bias, key_node, key_hot, key_pick = jax.random.split(key, 4)
    node_bias = jax.random.randint(key_bias, (N_NODE,), 0, 2 ** 19)
    node_rand = jax.random.randint(key_node, (TOKENS, N_NODE), 0, 2 ** 20)
    hot_held = jax.random.randint(key_hot, (groups,), 0, N_NODE * N_DP)
    hot_node = hot_held // N_DP
    hot_id = hot_node * NODE_EXPERTS + hot_held % N_DP
    token_ids = jnp.arange(TOKENS, dtype=jnp.int32)
    group_ids = token_ids // TOK
    first_rows = token_ids % TOK < CAP
    node_ids = jnp.arange(N_NODE, dtype=jnp.int32)
    force_node = first_rows[:, None] & (node_ids[None, :] == hot_node[group_ids][:, None])
    node_score = (node_rand + node_bias[None, :] + force_node.astype(jnp.int32) * 2 ** 22) * N_NODE + node_ids[None, :]
    chosen = jnp.argsort(-node_score, axis=1, stable=True)[:, :NODE_LIMIT]
    width = NODE_LIMIT * NODE_EXPERTS
    candidates = (chosen[:, :, None] * NODE_EXPERTS + jnp.arange(NODE_EXPERTS, dtype=jnp.int32)[None, None, :]).reshape(TOKENS, width)
    pick_rand = jax.random.randint(key_pick, (TOKENS, width), 0, 2 ** 20)
    force_pick = first_rows[:, None] & (candidates == hot_id[group_ids][:, None])
    pick_score = (pick_rand + force_pick.astype(jnp.int32) * 2 ** 22) * width + jnp.arange(width, dtype=jnp.int32)[None, :]
    order = jnp.argsort(-pick_score, axis=1, stable=True)[:, :TOPK]
    expert_ids = jnp.take_along_axis(candidates, order, axis=1).astype(jnp.int32)
    inner = expert_ids % NODE_EXPERTS
    in_window = inner < N_DP
    held = expert_ids // NODE_EXPERTS * N_DP + inner
    onehot = ((held[:, :, None] == jnp.arange(N_NODE * N_DP, dtype=jnp.int32)[None, None, :]) & in_window[:, :, None]).astype(jnp.int32)
    onehot = onehot.reshape(groups, TOK * TOPK, N_NODE * N_DP)
    counts = jnp.cumsum(onehot, axis=1) - onehot
    ranks = jnp.sum(counts * onehot, axis=2).reshape(TOKENS, TOPK)
    slots = jnp.where(in_window & (ranks < CAP), ranks, -1).astype(jnp.int32)
    return (expert_ids, slots)


def draw_route_expert(key, part):
    expert_ids, slots = routing(key)
    return expert_ids


def draw_route_slot(key, part):
    expert_ids, slots = routing(key)
    return slots


def block_scale(stream_key, dims, cuts, low, high):
    gain, own = 1.0, jax.random.fold_in(stream_key, 6)
    for dim, blocks in cuts:
        draws = jnp.exp(jax.random.uniform(jax.random.fold_in(own, dim), (blocks,), jnp.float32, low / len(cuts), high / len(cuts)))
        gain = gain * jnp.repeat(draws, dims[dim] // blocks).reshape([-1 if axis == dim else 1 for axis in range(len(dims))])
    return gain


def centred(stream_key, shape, scale, reach, cuts=(), held_as=jnp.bfloat16):
    factor_of = block_scale(stream_key, shape, cuts, -0.22, 0.18) if cuts else 1.0
    entries = jax.random.normal(stream_key, shape, jnp.float32) * scale * factor_of
    return jnp.minimum(jnp.maximum(entries, -reach), reach).astype(held_as)


def setup_inputs(seed: int = 0) -> dict:
    key_of = jax.random.split(jax.random.key(seed), 12)
    layer_input = centred(key_of[0], (TOKENS, D), 1.0, 6.0, ((0, 16), (1, 2)))
    grad_out = centred(key_of[1], (TOKENS, D), 1.0, 6.0, ((0, 16), (1, 2)))
    gate_values = jnp.clip(0.049804688 + 0.4501953 * jax.random.uniform(key_of[2], (TOKENS, TOPK), jnp.float32) ** block_scale(key_of[2], (TOKENS, TOPK), ((0, 16),), -0.2, 0.2), 0.049804688, 0.5).astype(jnp.bfloat16)
    route_expert = draw_route_expert(jax.random.fold_in(key_of[11], 71), 0)
    route_slot = draw_route_slot(jax.random.fold_in(key_of[11], 71), 0)
    shared_gate = centred(key_of[5], (FS, D), D ** -0.5, 0.125, ((0, 2), (1, 4)))
    shared_up = centred(key_of[6], (FS, D), D ** -0.5, 0.125, ((0, 2), (1, 4)))
    shared_down = centred(key_of[7], (FS, D), FS ** -0.5, 0.15625, ((0, 2), (1, 4)))
    expert_gate = centred(key_of[8], (EXPERTS, FR, D), D ** -0.5, 0.125, ((0, 16), (1, 2)))
    expert_up = centred(key_of[9], (EXPERTS, FR, D), D ** -0.5, 0.125, ((0, 16), (1, 2)))
    expert_down = centred(key_of[10], (EXPERTS, FR, D), FR ** -0.5, 0.21875, ((0, 16), (1, 2)))
    return {"layer_input": layer_input, "grad_out": grad_out, "gate_values": gate_values, "route_expert": route_expert, "route_slot": route_slot, "shared_gate": shared_gate, "shared_up": shared_up, "shared_down": shared_down, "expert_gate": expert_gate, "expert_up": expert_up, "expert_down": expert_down}


def reference(layer_input, grad_out, gate_values, route_expert, route_slot, shared_gate, shared_up, shared_down, expert_gate, expert_up, expert_down):
    groups = N_NODE * N_DP
    shared_a = jnp.dot(layer_input, shared_gate.T, preferred_element_type=jnp.float32)
    shared_b = jnp.dot(layer_input, shared_up.T, preferred_element_type=jnp.float32)
    sigm_a = jax.nn.sigmoid(shared_a)
    silu_a = shared_a * sigm_a
    shared_h = (silu_a * shared_b).astype(jnp.bfloat16)
    shared_e = jnp.dot(grad_out, shared_down.T, preferred_element_type=jnp.float32)
    shared_da = (shared_e * shared_b * sigm_a * (1.0 + shared_a * (1.0 - sigm_a))).astype(jnp.bfloat16)
    shared_db = (shared_e * silu_a).astype(jnp.bfloat16)

    slice_width = FS // N_LOCAL
    shared_dx = jnp.zeros((TOKENS, D), jnp.float32)
    for piece in range(N_LOCAL):
        lower = piece * slice_width
        upper = lower + slice_width
        term = jnp.dot(shared_da[:, lower:upper], shared_gate[lower:upper, :], preferred_element_type=jnp.float32)
        term = term + jnp.dot(shared_db[:, lower:upper], shared_up[lower:upper, :], preferred_element_type=jnp.float32)
        shared_dx = shared_dx + term.astype(jnp.bfloat16).astype(jnp.float32)

    def group_step(carry, items):
        x_group, dy_group, da_group, db_group, h_group = items
        part_gate = jnp.dot(da_group.T, x_group, preferred_element_type=jnp.float32)
        part_up = jnp.dot(db_group.T, x_group, preferred_element_type=jnp.float32)
        part_down = jnp.dot(h_group.T, dy_group, preferred_element_type=jnp.float32)
        carry = (carry[0] + part_gate.astype(jnp.bfloat16).astype(jnp.float32),
                 carry[1] + part_up.astype(jnp.bfloat16).astype(jnp.float32),
                 carry[2] + part_down.astype(jnp.bfloat16).astype(jnp.float32))
        return carry, None

    start_sums = (jnp.zeros((FS, D), jnp.float32), jnp.zeros((FS, D), jnp.float32), jnp.zeros((FS, D), jnp.float32))
    items = (layer_input.reshape(groups, TOK, D), grad_out.reshape(groups, TOK, D), shared_da.reshape(groups, TOK, FS),
             shared_db.reshape(groups, TOK, FS), shared_h.reshape(groups, TOK, FS))
    sums, unused = lax.scan(group_step, start_sums, items)
    grad_shared_gate = sums[0].astype(jnp.bfloat16)
    grad_shared_up = sums[1].astype(jnp.bfloat16)
    grad_shared_down = sums[2].astype(jnp.bfloat16)

    block_rows = groups * CAP
    kept = route_slot >= 0
    held = (route_expert // NODE_EXPERTS) * N_DP + route_expert % NODE_EXPERTS
    token_ids = jnp.arange(TOKENS, dtype=jnp.int32)
    group_ids = (token_ids // TOK)[:, None]
    position = held * block_rows + group_ids * CAP + route_slot
    position = jnp.where(kept, position, EXPERTS * block_rows).astype(jnp.int32)
    flat_ids = jnp.arange(TOKENS * TOPK, dtype=jnp.int32)
    table = jnp.full((EXPERTS * block_rows,), TOKENS * TOPK, jnp.int32)
    table = table.at[position.reshape(-1)].set(flat_ids, mode="drop").reshape(EXPERTS, block_rows)

    x_padded = jnp.concatenate([layer_input, jnp.zeros((1, D), layer_input.dtype)], axis=0)
    dy_padded = jnp.concatenate([grad_out, jnp.zeros((1, D), grad_out.dtype)], axis=0)
    gate_padded = jnp.concatenate([gate_values.reshape(-1), jnp.zeros((1,), gate_values.dtype)], axis=0)

    def expert_step(carry, items):
        dx_total, gate_total = carry
        choice_ids, weight_gate, weight_up, weight_down = items
        token_rows = choice_ids // TOPK
        rows_x = x_padded[token_rows]
        rows_dy = dy_padded[token_rows]
        weight_q = gate_padded[choice_ids].astype(jnp.float32)[:, None]
        pre_a = jnp.dot(rows_x, weight_gate.T, preferred_element_type=jnp.float32)
        pre_b = jnp.dot(rows_x, weight_up.T, preferred_element_type=jnp.float32)
        back_e = jnp.dot(rows_dy, weight_down.T, preferred_element_type=jnp.float32)
        sigm_b = jax.nn.sigmoid(pre_a)
        silu_b = pre_a * sigm_b
        hidden = silu_b * pre_b
        gate_grad = jnp.sum(back_e * hidden, axis=1)
        grad_a = (weight_q * back_e * pre_b * sigm_b * (1.0 + pre_a * (1.0 - sigm_b))).astype(jnp.bfloat16)
        grad_b = (weight_q * back_e * silu_b).astype(jnp.bfloat16)
        hidden_q = (weight_q * hidden).astype(jnp.bfloat16)
        new_gate = jnp.dot(grad_a.T, rows_x, preferred_element_type=jnp.float32).astype(jnp.bfloat16)
        new_up = jnp.dot(grad_b.T, rows_x, preferred_element_type=jnp.float32).astype(jnp.bfloat16)
        new_down = jnp.dot(hidden_q.T, rows_dy, preferred_element_type=jnp.float32).astype(jnp.bfloat16)
        row_dx = jnp.dot(grad_a, weight_gate, preferred_element_type=jnp.float32)
        row_dx = row_dx + jnp.dot(grad_b, weight_up, preferred_element_type=jnp.float32)
        dx_total = dx_total.at[token_rows].add(row_dx)
        gate_total = gate_total.at[choice_ids].set(gate_grad)
        return (dx_total, gate_total), (new_gate, new_up, new_down)

    start_carry = (jnp.zeros((TOKENS + 1, D), jnp.float32), jnp.zeros((TOKENS * TOPK + 1,), jnp.float32))
    carry, weights_out = lax.scan(expert_step, start_carry, (table, expert_gate, expert_up, expert_down))
    routed_dx = carry[0][:TOKENS]
    grad_gates = carry[1][:TOKENS * TOPK].reshape(TOKENS, TOPK)
    grad_x = (shared_dx + routed_dx).astype(jnp.bfloat16)
    return (grad_x, grad_gates, grad_shared_gate, grad_shared_up, grad_shared_down,
            weights_out[0], weights_out[1], weights_out[2])
```

```python
import functools

import jax
import jax.numpy as jnp
from jax import lax
from jax.experimental import pallas as pl
from jax.experimental.pallas import tpu as pltpu
from jax.sharding import PartitionSpec as P

NODE_EXPERTS = 10
BLOCK = 8
GATE_ROW = 6
CORE, ALIGNED, LOCAL, MIDDLE = range(4)
VMEM_BYTES = 24 * 1024 * 1024
LINE_BYTES = 8 * 1024 * 1024
BF = jnp.bfloat16
F32 = jnp.float32

SMEM = pl.BlockSpec(memory_space=pltpu.SMEM)
VMEM = pl.BlockSpec(memory_space=pltpu.VMEM)
ANY = pl.BlockSpec(memory_space=pl.ANY)


def dot_rows(left, right):
    return lax.dot_general(left, right, (((0,), (0,)), ((), ())), preferred_element_type=F32)


def dot_cols(left, right):
    return lax.dot_general(left, right, (((1,), (1,)), ((), ())), preferred_element_type=F32)


def dot(left, right):
    return lax.dot_general(left, right, (((1,), (0,)), ((), ())), preferred_element_type=F32)


def whole(dims):
    zeros = (0,) * len(dims)
    return pl.BlockSpec(dims, lambda i: zeros)


def far(value):
    return ("far", pltpu.with_memory_space_constraint(value, pltpu.HBM))


def call(kernel, outs, operands, name, flags=(), after=(), held=(), vmem=VMEM_BYTES, far_outs=()):
    count = len(flags) + len(operands)
    first = count + len(after)

    def body(*refs):
        kernel(*refs[:count], *refs[first + len(held) : len(refs) - len(held)])

    specs = [whole(v[1].shape) if isinstance(v, tuple) else VMEM for v in operands]
    operands = [v[1] if isinstance(v, tuple) else v for v in operands]
    got = pl.pallas_call(
        body,
        grid=(1,),
        out_shape=[pltpu.HBM(v.shape, v.dtype) if i in far_outs else v for i, v in enumerate(outs)]
        + [shape(v.shape, v.dtype) for v in held],
        in_specs=[SMEM] * len(flags) + specs + [ANY] * (len(after) + len(held)),
        out_specs=[whole(v.shape) if i in far_outs else VMEM for i, v in enumerate(outs)]
        + [ANY] * len(held),
        input_output_aliases={first + i: len(outs) + i for i in range(len(held))},
        compiler_params=pltpu.CompilerParams(vmem_limit_bytes=vmem),
        cost_estimate=pl.CostEstimate(flops=0, bytes_accessed=0, transcendentals=0),
        name=name,
    )(*flags, *operands, *after, *held)
    return list(got)


def shape(dims, dtype):
    return jax.ShapeDtypeStruct(dims, dtype)


def positions(expert, slot, n_dp):
    node = (expert * 205) >> 11
    held = node * n_dp + expert - node * NODE_EXPERTS
    return jnp.where(slot >= 0, held * BLOCK + slot, -1)


def pack_kernel(*refs):
    rows = refs[0].shape[0]
    for index, ref in enumerate(refs[:-1]):
        refs[-1][index * rows : (index + 1) * rows] = ref[...]


def select_kernel(n_dp, expert_ref, slot_ref, gate_ref, x_ref, dy_ref, out_ref):
    choices, tokens = slot_ref.shape
    slots = out_ref.shape[0]
    width = x_ref.shape[1]
    line = lax.broadcasted_iota(jnp.int32, (slots, tokens), 0)
    pos = positions(expert_ref[...], slot_ref[...], n_dp)
    gate = gate_ref[...].astype(F32)
    sel = jnp.zeros((slots, tokens), F32)
    selq = jnp.zeros((slots, tokens), F32)
    for k in range(choices):
        hit = pos[k : k + 1] == line
        sel = jnp.where(hit, 1.0, sel)
        selq = jnp.where(hit, gate[k : k + 1], selq)
    out_ref[:, :width] = dot(sel.astype(BF), x_ref[...]).astype(BF)
    out_ref[:, width:] = dot(selq.astype(BF), dy_ref[...]).astype(BF)


def product_kernel(inputs, blocks, first, mats, flag_ref, *refs):
    source = refs[:inputs]
    own_ref, oth_ref, keep_ref, send_ref, mine_ref, *away = refs[inputs:]
    tokens, width = source[0].shape[0], keep_ref.shape[1]
    hidden = mine_ref.shape[1]
    core = flag_ref[CORE]
    for place, out in ((core, keep_ref), (1 - core, send_ref)):
        at = pl.ds(pl.multiple_of(place * width, 128), width)
        parts = [ref[:, at] for ref in source]
        if inputs > blocks:
            aligned = flag_ref[ALIGNED] == 1
            parts = [jnp.where(aligned, parts[0], parts[1]), jnp.where(aligned, parts[1], parts[2])]
        for j, part in enumerate(parts):
            out[j * tokens : (j + 1) * tokens] = part
    keep, send = keep_ref[...], send_ref[...]
    for index in range(mats):
        weight = slice((first + index) * hidden, (first + index + 1) * hidden)
        product = dot_cols(keep, own_ref[weight]) + dot_cols(send, oth_ref[weight])
        at = slice(index * tokens, (index + 1) * tokens)
        mine_ref[at] = product[:tokens]
        for j, ref in enumerate(away):
            ref[at] = product[(j + 1) * tokens : (j + 2) * tokens].astype(BF)


def slope_kernel(terms, *refs):
    def total(part):
        value = part[0][...]
        for ref in part[1:]:
            value = value + ref[...].astype(F32)
        return value

    both, e = total(refs[:terms]), total(refs[terms : 2 * terms])
    tokens = e.shape[0]
    a, b = both[:tokens], both[tokens:]
    sigm = jax.nn.sigmoid(a)
    silu = a * sigm
    values = (silu * b, e * b * sigm * (1.0 + a * (1.0 - sigm)), e * silu)
    for index, out in enumerate(refs[2 * terms :]):
        part = out.shape[1]
        for row, value in enumerate(values):
            out[row * tokens : (row + 1) * tokens] = value[:, index * part : (index + 1) * part].astype(BF)


def weight_grad_kernel(pieces, x_keep, x_recv, dy_keep, dy_recv, *refs):
    tokens = refs[0].shape[0] // 3
    x = jnp.concatenate([x_keep[...], x_recv[...]], axis=0)
    dy = jnp.concatenate([dy_keep[...], dy_recv[...]], axis=0)
    for index, ref in enumerate(refs[pieces:]):
        at = slice(index * tokens, (index + 1) * tokens)
        left = jnp.concatenate([piece[at] for piece in refs[:pieces]], axis=0)
        ref[...] = dot_rows(left, dy if index == 0 else x).astype(BF)


def shared_dx_kernel(blocks, halves, flag_ref, *refs):
    pieces = [refs[i * blocks : (i + 1) * blocks] for i in range(halves)]
    own_ref, oth_ref, *outs = refs[halves * blocks :]
    tokens = outs[0].shape[0]
    hidden, width = own_ref.shape[0] // 3, own_ref.shape[1]

    def collect(index):
        at = slice(index * tokens, (index + 1) * tokens)
        parts = [jnp.concatenate([ref[at] for ref in part], axis=0) for part in pieces]
        return jnp.concatenate(parts, axis=1)

    da, db = collect(1), collect(2)
    core = flag_ref[CORE]
    for place, ref in ((core, own_ref), (1 - core, oth_ref)):
        at = pl.ds(pl.multiple_of(place * width, 128), width)
        got = (dot(da, ref[:hidden]) + dot(db, ref[hidden : 2 * hidden])).astype(BF)
        parts = [got[j * tokens : (j + 1) * tokens] for j in range(blocks)]
        for j in range(blocks):
            outs[j][:, at] = parts[j]
        if len(outs) > blocks:
            outs[blocks][:, at] = jnp.where(flag_ref[ALIGNED] == 1, parts[1], parts[0])


def routed_kernel(pair, slices, waits, flag_ref, x_ref, dy_ref, gate_ref, up_ref, down_ref, *refs):
    new_gate, new_up, new_down, *refs = refs[waits:]
    outs, (acc, gate_acc, rows_x, rows_dy) = refs[:-4], refs[-4:]
    step = pl.program_id(0)
    slots, width = acc.shape
    piece = width // slices
    here = pl.ds(pl.multiple_of(flag_ref[LOCAL] * piece, 128), piece)
    there = pl.ds(pl.multiple_of((slices - 1 - flag_ref[LOCAL]) * piece, 128), piece)

    @pl.when(step == 0)
    def _():
        if pair:
            rows_x[:, here] = x_ref[:, :piece]
            rows_dy[:, here] = x_ref[:, piece:]
            rows_x[:, there] = dy_ref[:, :piece]
            rows_dy[:, there] = dy_ref[:, piece:]
        else:
            rows_x[...] = x_ref[...]
            rows_dy[...] = dy_ref[...]

    x = rows_x[...]
    dy = rows_dy[...]
    w_gate, w_up, w_down = gate_ref[0], up_ref[0], down_ref[0]
    pre_a = dot_cols(x, w_gate)
    pre_b = dot_cols(x, w_up)
    back_e = dot_cols(dy, w_down)
    sigm = jax.nn.sigmoid(pre_a)
    silu = pre_a * sigm
    hidden = silu * pre_b
    part = jnp.sum(back_e * hidden, axis=1, keepdims=True)
    grad_a = (back_e * pre_b * sigm * (1.0 + pre_a * (1.0 - sigm))).astype(BF)
    grad_b = (back_e * silu).astype(BF)
    row = dot(grad_a, w_gate) + dot(grad_b, w_up)
    new_gate[0] = dot_rows(grad_a, x).astype(BF)
    new_up[0] = dot_rows(grad_b, x).astype(BF)
    new_down[0] = dot_rows(hidden.astype(BF), dy).astype(BF)

    @pl.when(step == 0)
    def _():
        acc[...] = row
        gate_acc[...] = part

    @pl.when(step > 0)
    def _():
        acc[...] += row
        gate_acc[...] += part

    @pl.when(step == pl.num_programs(0) - 1)
    def _():
        lane = lax.broadcasted_iota(jnp.int32, (slots, 128), 1)
        sub = lax.broadcasted_iota(jnp.int32, (slots, 128), 0) % BLOCK
        spread = jnp.where(lane == sub, gate_acc[...], 0.0).reshape(slots // BLOCK, BLOCK, 128)
        line = jnp.sum(spread, axis=1, keepdims=True)
        line = jnp.broadcast_to(line, spread.shape).reshape(slots, 128)
        line = jnp.where(sub == GATE_ROW, line, 0.0)
        for index in range(slices):
            start = index * piece
            acc[:, start : start + 128] += line
        if pair:
            outs[0][...] = acc[:, here].astype(BF)
            outs[1][...] = acc[:, there].astype(BF)
        else:
            outs[0][...] = acc[...].astype(BF)


def combine_kernel(n_dp, flag_ref, expert_ref, slot_ref, gate_ref, rows_ref, *refs):
    dx_ref, gates_ref = refs[-2:]
    choices, tokens = slot_ref.shape
    slots = rows_ref.shape[0]
    line = lax.broadcasted_iota(jnp.int32, (slots, tokens), 0)
    sub = lax.broadcasted_iota(jnp.int32, (128, tokens), 0)
    pos = positions(expert_ref[...], slot_ref[...], n_dp)
    gate = gate_ref[...].astype(F32)
    rows = rows_ref[...]
    sel = jnp.zeros((slots, tokens), F32)
    for k in range(choices):
        at = pos[k : k + 1]
        sel = jnp.where(at == line, 1.0, sel)
        slot = at & (BLOCK - 1)
        pick = jnp.where((at >= 0) & (line == at - slot + GATE_ROW), 1.0, 0.0).astype(BF)
        found = dot_rows(rows[:, :128], pick)
        value = jnp.sum(jnp.where(sub == slot, found, 0.0), axis=0, keepdims=True)
        gates_ref[k : k + 1] = value / gate[k : k + 1]
    total = dot_rows(sel.astype(BF), rows)
    terms = refs[:-2]
    if len(terms) == 3:
        second = jnp.where(flag_ref[ALIGNED] == 1, terms[1][...], terms[2][...])
        total = total + terms[0][...].astype(F32) + second.astype(F32)
    else:
        total = total + terms[0][...].astype(F32)
    dx_ref[...] = total.astype(BF)


def add_kernel(own_ref, came_ref, out_ref):
    out_ref[...] = (own_ref[...].astype(F32) + came_ref[...].astype(F32)).astype(BF)


def total_kernel(flag_ref, own_ref, came_ref, next_ref, out_ref, pay_ref):
    total = (own_ref[...].astype(F32) + came_ref[...].astype(F32)).astype(BF)
    out_ref[...] = total
    pay_ref[...] = jnp.where(flag_ref[MIDDLE] == 1, total, next_ref[...])


def line_sum(value, n_node, depth):
    half = n_node // 2
    if n_node % 2:
        return lax.psum(value, "node")
    for k in range(half - 1):
        pairs = [(k, k + 1), (n_node - 1 - k, n_node - 2 - k)]
        got = lax.ppermute(value, "node", pairs)
        value = (value.astype(F32) + got.astype(F32)).astype(BF)
    got = lax.ppermute(value, "node", [(half - 1, half), (half, half - 1)])
    value = (value.astype(F32) + got.astype(F32)).astype(BF)
    for k in reversed(range(half - 1)):
        pairs = [(k + 1, k), (n_node - 2 - k, n_node - 1 - k)]
        got = lax.ppermute(value, "node", pairs)
        value = jnp.where(depth == k, got, value)
    return value


INWARD, CENTRE, OUTWARD = [(0, 1), (3, 2)], [(1, 2), (2, 1)], [(1, 0), (2, 3)]


class LineOfFour:
    def __init__(self, flags):
        self.flags = flags
        self.values, self.outer, self.sums, self.across, self.totals, self.ends = [], [], [], [], [], []
        self.last = []

    def add(self, values):
        self.values += values
        for value in self.values[len(self.outer) : 2]:
            self.outer.append(lax.ppermute(value, "node", INWARD))

    def step(self, kernel, name, operands, outs, after=(), held=(), flags=()):
        like = [shape(operands[0].shape, BF)] * outs
        got = call(kernel, like, operands, name, flags, self.last + list(after), held, LINE_BYTES)
        self.last = got[:1]
        return got

    def sum(self, after=()):
        now = len(self.sums)
        ahead = self.values[2:3] if now == 0 else []
        got = self.step(add_kernel, "line_sum", [self.values[now], self.outer[now]], 1, after, ahead)
        if ahead:
            self.values[2] = got[1]
            self.outer.append(lax.ppermute(got[1], "node", INWARD))
        self.sums.append(got[0])
        self.across.append(lax.ppermute(got[0], "node", CENTRE))

    def total(self, after=(), held=()):
        back = len(self.totals)
        operands = [self.sums[back], self.across[back]]
        waits = list(after) + (self.ends[back - 2 : back - 1] if back > 1 else [])
        if back + 3 < len(self.values):
            operands.append(self.values[back + 3])
            got = self.step(total_kernel, "line_total", operands, 2, waits, held, [self.flags])
            came = lax.ppermute(got[1], "node", INWARD + OUTWARD)
            self.outer.append(came)
            held = got[2:]
        else:
            got = self.step(add_kernel, "line_total", operands, 1, waits, held)
            came = lax.ppermute(got[0], "node", OUTWARD)
            held = got[1:]
        self.totals.append(got[0])
        self.ends.append(came)
        return list(held)

    def finish(self, middle):
        while len(self.sums) < len(self.values):
            self.sum()
        while len(self.totals) < len(self.values):
            self.total()
        return [jnp.where(middle, a, b) for a, b in zip(self.totals, self.ends)]


def on_device(
    layer_input,
    grad_out,
    gate_values,
    route_expert,
    route_slot,
    shared_gate,
    shared_up,
    shared_down,
    expert_gate,
    expert_up,
    expert_down,
):
    n_node = lax.axis_size("node")
    n_local = lax.axis_size("local")
    n_dp = lax.axis_size("dp")
    outer = n_dp // 2
    groups = n_node * n_dp
    slots = groups * BLOCK
    tokens, feat = layer_input.shape
    hidden_s, width = shared_gate.shape
    hidden_r, model = expert_gate.shape[1:]
    local = lax.axis_index("local")
    dp = lax.axis_index("dp")
    node = lax.axis_index("node")
    row, core = dp // 2, dp % 2
    paired = n_local == 2 and outer == 2
    middle = (node == 1) | (node == 2)
    flags = jnp.stack([core, row == local, local, middle]).astype(jnp.int32)

    swap_core = [(d, d ^ 1) for d in range(n_dp)]

    def outer_shift(step):
        return [(d, (d + 2 * step) % n_dp) for d in range(n_dp)]

    def at(l, y, c):
        return l * n_dp + 2 * y + c

    straight, diagonal = [], []
    if paired:
        for l in range(2):
            for c in range(2):
                straight.append((at(l, l, c), at(1 - l, l, c)))
                straight.append((at(l, 1 - l, c), at(l, l, c)))
                diagonal.append((at(l, 1 - l, c), at(1 - l, l, c)))
    backwards = [(b, a) for a, b in straight]

    def core_swap(value):
        return lax.ppermute(value, "dp", swap_core)

    def feature_blocks(own):
        if paired:
            first = lax.ppermute(own, ("local", "dp"), straight)
            second = lax.ppermute(own, ("local", "dp"), diagonal)
            return [own, first, second]
        full = lax.all_gather(own, "local", axis=1, tiled=True)
        found = [lax.dynamic_slice_in_dim(full, row * 2 * width, 2 * width, axis=1)]
        for step in range(1, outer):
            there = (row + outer - step) % outer
            piece = lax.dynamic_slice_in_dim(full, there * 2 * width, 2 * width, axis=1)
            found.append(lax.ppermute(piece, "dp", outer_shift(outer - step)))
        return found

    def gather_groups(value):
        near = [value]
        for step in range(1, outer):
            near.append(lax.ppermute(value, "dp", outer_shift(outer - step)))
        return near + [core_swap(v) for v in near]

    gate_values, route_expert, route_slot = gate_values.T, route_expert.T, route_slot.T
    x_blocks = feature_blocks(layer_input)
    dy_blocks = feature_blocks(grad_out)
    weights = [shared_gate, shared_up, shared_down]
    (shared,) = call(pack_kernel, [shape((3 * hidden_s, width), BF)], [far(v) for v in weights], "pack_weights")
    shared_oth = core_swap(shared)

    (send_rows,) = call(
        functools.partial(select_kernel, n_dp),
        [shape((slots, 2 * feat), BF)],
        [far(v) for v in (route_expert, route_slot, gate_values, layer_input, grad_out)],
        "select_rows",
        after=[shared_oth],
    )
    back_rows = lax.all_to_all(
        send_rows.reshape(groups, BLOCK, 2 * feat),
        ("node", "dp"),
        split_axis=0,
        concat_axis=0,
        tiled=True,
    ).reshape(slots, 2 * feat)

    halves = 2 if hidden_s % 256 == 0 else 1
    part = hidden_s // halves

    def partial(blocks, weight, oth, first, mats, name, after):
        x_keep, x_send, *got = call(
            functools.partial(product_kernel, len(blocks), outer, first, mats),
            [shape((outer * tokens, width), BF)] * 2
            + [shape((mats * tokens, hidden_s), F32)]
            + [shape((mats * tokens, hidden_s), BF)] * (outer - 1),
            ([far(blocks[0])] + blocks[1:] if paired else blocks) + [weight, oth],
            name,
            [flags],
            after,
            far_outs=(0, 1),
        )
        sums = [got[0]]
        for step in range(1, outer):
            sums.append(lax.ppermute(got[step], "dp", outer_shift(step)))
        return x_keep, core_swap(x_send), sums

    x_keep, x_recv, ab_sums = partial(x_blocks, shared, shared_oth, 0, 2, "shared_ab", [send_rows])
    dy_keep, dy_recv, e_sums = partial(
        dy_blocks, shared, shared_oth, 2, 1, "shared_e", ab_sums[:1]
    )
    values = call(
        functools.partial(slope_kernel, len(e_sums)),
        [shape((3 * tokens, part), BF)] * halves,
        ab_sums + e_sums,
        "shared_slopes",
        after=[x_recv, dy_recv],
    )
    pair = n_local == 2
    swap_local = [(0, 1), (1, 0)]
    if pair:
        row_operands = [back_rows, lax.ppermute(back_rows, "local", swap_local)]
    else:
        row_operands = [
            lax.all_gather(back_rows[:, :feat], "local", axis=1, tiled=True),
            lax.all_gather(back_rows[:, feat:], "local", axis=1, tiled=True),
        ]

    def weight_grads(pieces, after):
        rows = [x_keep, x_recv, dy_keep, dy_recv]
        return call(
            functools.partial(weight_grad_kernel, len(pieces)),
            [shape((part, width), BF)] * 3,
            [far(v) for v in rows] + pieces,
            "shared_weight_grads",
            after=after,
        )

    line = LineOfFour(flags) if n_node == 4 else None
    slopes = [gather_groups(values[0])]
    parts = weight_grads(slopes[0], row_operands[1:])
    if line:
        line.add(parts)
        parts = line.values

    row_outs = [shape((slots, feat), BF)] * 2 if pair else [shape((slots, model), BF)]
    waits = parts[:1]
    block = hidden_r // 2 if hidden_r % 128 == 0 else hidden_r
    tile = pl.BlockSpec((1, block, model), lambda i: (0, i, 0))
    experts = [far(v)[1] for v in (expert_gate, expert_up, expert_down)]
    new_gate, new_up, new_down, *rows_out = pl.pallas_call(
        functools.partial(routed_kernel, pair, n_local, len(waits)),
        grid=(hidden_r // block,),
        out_shape=[pltpu.HBM((1, hidden_r, model), BF)] * 3 + row_outs,
        in_specs=[SMEM]
        + [VMEM] * len(row_operands)
        + [tile, tile, tile]
        + [ANY] * len(waits),
        out_specs=[tile, tile, tile] + [VMEM] * len(row_outs),
        scratch_shapes=[
            pltpu.VMEM((slots, model), F32),
            pltpu.VMEM((slots, 1), F32),
            pltpu.VMEM((slots, model), BF),
            pltpu.VMEM((slots, model), BF),
        ],
        compiler_params=pltpu.CompilerParams(vmem_limit_bytes=VMEM_BYTES),
        cost_estimate=pl.CostEstimate(flops=0, bytes_accessed=0, transcendentals=0),
        name="routed_expert",
    )(flags, *row_operands, *experts, *waits)
    if pair:
        mine, gone = rows_out
        came = lax.ppermute(gone, "local", swap_local)
        row_sum = (mine.astype(F32) + came.astype(F32)).astype(BF)
    else:
        row_sum = lax.psum_scatter(rows_out[0], "local", scatter_dimension=1, tiled=True)
    for value in values[1:]:
        (value,) = call(lambda: None, [], [], "hold", after=slopes[-1][1:outer], held=[value])
        slopes.append(gather_groups(value))
        more = weight_grads(slopes[-1], rows_out[:1])
        if line:
            line.add(more)
        else:
            parts = parts + more
    if line:
        line.sum(rows_out[:1])
        line.sum()
        line.total()
    dx_blocks = call(
        functools.partial(shared_dx_kernel, outer, halves),
        [shape((tokens, 2 * width), BF)] * (outer + (1 if paired else 0)),
        sum((pieces[:outer] for pieces in slopes), []) + [shared, shared_oth],
        "shared_dx",
        [flags],
        line.last if line else (),
    )
    if line:
        line.sum(dx_blocks[:1])
        dx_blocks = line.total(held=dx_blocks)
        line.sum()
        line.total()
        line.sum()
        (row_sum,) = line.total(held=[row_sum])
    home = lax.all_to_all(
        row_sum.reshape(groups, BLOCK, feat),
        ("node", "dp"),
        split_axis=0,
        concat_axis=0,
        tiled=True,
    ).reshape(slots, feat)
    if line:
        line.sum()
        line.total()
    if paired:
        mine, other, straight_pay = dx_blocks
        first = lax.ppermute(straight_pay, ("local", "dp"), backwards)
        second = lax.ppermute(other, ("local", "dp"), diagonal)
        dx_terms = [first, mine, second]
    else:
        full = jnp.zeros((tokens, model), BF)
        for step, piece in enumerate(dx_blocks):
            if step:
                piece = lax.ppermute(piece, "dp", outer_shift(step))
            there = (row + outer - step) % outer
            full = lax.dynamic_update_slice_in_dim(full, piece, there * 2 * width, axis=1)
        dx_terms = [lax.psum_scatter(full, "local", scatter_dimension=1, tiled=True)]
    grad_x, grad_gates = call(
        functools.partial(combine_kernel, n_dp),
        [shape((tokens, feat), BF), shape(route_slot.shape, F32)],
        [far(v) for v in [route_expert, route_slot, gate_values, home] + dx_terms],
        "combine",
        [flags],
        line.last if line else (),
        far_outs=(0, 1),
    )
    if line:
        line.total([grad_x])
        parts = line.finish(middle)
    else:
        depth = jnp.minimum(node, n_node - 1 - node)
        parts = [line_sum(value, n_node, depth) for value in parts]
    grad_down, grad_gate, grad_up = (
        jnp.concatenate(parts[i::3], axis=0) if halves > 1 else parts[i] for i in range(3)
    )
    if n_local > 2:
        grad_gates = lax.psum(jnp.where(local == 0, grad_gates, 0.0), "local")
    return grad_x, grad_gates.T, grad_gate, grad_up, grad_down, new_gate, new_up, new_down


def solution(mesh):
    tokens = P(("node", "dp"), "local")
    choices = P(("node", "dp"), None)
    shared = P("local", "dp")
    expert = P(("node", "dp"), "local", None)
    return jax.shard_map(
        on_device,
        mesh=mesh,
        in_specs=(tokens, tokens, choices, choices, choices) + (shared,) * 3 + (expert,) * 3,
        out_specs=(tokens, choices) + (shared,) * 3 + (expert,) * 3,
        check_vma=False,
    )
```

```python
import functools

import jax
import jax.numpy as jnp
from jax import lax
from jax.experimental import pallas as pl
from jax.experimental.pallas import tpu as pltpu
from jax.sharding import PartitionSpec as P

NODE_EXPERTS = 10
BLOCK = 8
GATE_ROW = 6
CORE, ALIGNED, LOCAL, MIDDLE = range(4)
VMEM_BYTES = 16 * 1024 * 1024
LINE_BYTES = 8 * 1024 * 1024
BF = jnp.bfloat16
F32 = jnp.float32

SMEM = pl.BlockSpec(memory_space=pltpu.SMEM)
VMEM = pl.BlockSpec(memory_space=pltpu.VMEM)
ANY = pl.BlockSpec(memory_space=pl.ANY)


def dot_rows(left, right):
    return lax.dot_general(left, right, (((0,), (0,)), ((), ())), preferred_element_type=F32)


def dot_cols(left, right):
    return lax.dot_general(left, right, (((1,), (1,)), ((), ())), preferred_element_type=F32)


def dot(left, right):
    return lax.dot_general(left, right, (((1,), (0,)), ((), ())), preferred_element_type=F32)


def whole(dims):
    zeros = (0,) * len(dims)
    return pl.BlockSpec(dims, lambda i: zeros)


def far(value):
    return ("far", pltpu.with_memory_space_constraint(value, pltpu.HBM))


def call(kernel, outs, operands, name, flags=(), after=(), held=(), vmem=VMEM_BYTES, far_outs=()):
    count = len(flags) + len(operands)
    first = count + len(after)

    def body(*refs):
        kernel(*refs[:count], *refs[first + len(held) : len(refs) - len(held)])

    specs = [whole(v[1].shape) if isinstance(v, tuple) else VMEM for v in operands]
    operands = [v[1] if isinstance(v, tuple) else v for v in operands]
    after = [v[1] if isinstance(v, tuple) else v for v in after]
    got = pl.pallas_call(
        body,
        grid=(1,),
        out_shape=[pltpu.HBM(v.shape, v.dtype) if i in far_outs else v for i, v in enumerate(outs)]
        + [shape(v.shape, v.dtype) for v in held],
        in_specs=[SMEM] * len(flags) + specs + [ANY] * (len(after) + len(held)),
        out_specs=[whole(v.shape) if i in far_outs else VMEM for i, v in enumerate(outs)]
        + [ANY] * len(held),
        input_output_aliases={first + i: len(outs) + i for i in range(len(held))},
        compiler_params=pltpu.CompilerParams(vmem_limit_bytes=vmem),
        cost_estimate=pl.CostEstimate(flops=0, bytes_accessed=0, transcendentals=0),
        name=name,
    )(*flags, *operands, *after, *held)
    return list(got)


def shape(dims, dtype):
    return jax.ShapeDtypeStruct(dims, dtype)


def positions(expert, slot, n_dp):
    node = (expert * 205) >> 11
    held = node * n_dp + expert - node * NODE_EXPERTS
    return jnp.where(slot >= 0, held * BLOCK + slot, -1)


def pack_kernel(*refs):
    rows = refs[0].shape[0]
    for index, ref in enumerate(refs[:-1]):
        refs[-1][index * rows : (index + 1) * rows] = ref[...]


def select_kernel(n_dp, expert_ref, slot_ref, gate_ref, x_ref, dy_ref, out_ref):
    choices, tokens = slot_ref.shape
    slots = out_ref.shape[0]
    width = x_ref.shape[1]
    line = lax.broadcasted_iota(jnp.int32, (slots, tokens), 0)
    pos = positions(expert_ref[...], slot_ref[...], n_dp)
    gate = gate_ref[...].astype(F32)
    sel = jnp.zeros((slots, tokens), F32)
    selq = jnp.zeros((slots, tokens), F32)
    for k in range(choices):
        hit = pos[k : k + 1] == line
        sel = jnp.where(hit, 1.0, sel)
        selq = jnp.where(hit, gate[k : k + 1], selq)
    out_ref[:, :width] = dot(sel.astype(BF), x_ref[...]).astype(BF)
    out_ref[:, width:] = dot(selq.astype(BF), dy_ref[...]).astype(BF)


def product_kernel(inputs, blocks, first, mats, flag_ref, *refs):
    source = refs[:inputs]
    own_ref, oth_ref, keep_ref, send_ref, mine_ref, *away = refs[inputs:]
    tokens, width = source[0].shape[0], keep_ref.shape[1]
    hidden = mine_ref.shape[1]
    core = flag_ref[CORE]
    for place, out in ((core, keep_ref), (1 - core, send_ref)):
        at = pl.ds(pl.multiple_of(place * width, 128), width)
        parts = [ref[:, at] for ref in source]
        if inputs > blocks:
            aligned = flag_ref[ALIGNED] == 1
            parts = [jnp.where(aligned, parts[0], parts[1]), jnp.where(aligned, parts[1], parts[2])]
        for j, part in enumerate(parts):
            out[j * tokens : (j + 1) * tokens] = part
    keep, send = keep_ref[...], send_ref[...]
    for index in range(mats):
        weight = slice((first + index) * hidden, (first + index + 1) * hidden)
        product = dot_cols(keep, own_ref[weight]) + dot_cols(send, oth_ref[weight])
        at = slice(index * tokens, (index + 1) * tokens)
        mine_ref[at] = product[:tokens]
        for j, ref in enumerate(away):
            ref[at] = product[(j + 1) * tokens : (j + 2) * tokens].astype(BF)


def slope_kernel(terms, *refs):
    def total(part):
        value = part[0][...]
        for ref in part[1:]:
            value = value + ref[...].astype(F32)
        return value

    both, e = total(refs[:terms]), total(refs[terms : 2 * terms])
    tokens = e.shape[0]
    a, b = both[:tokens], both[tokens:]
    sigm = jax.nn.sigmoid(a)
    silu = a * sigm
    values = (silu * b, e * b * sigm * (1.0 + a * (1.0 - sigm)), e * silu)
    for index, out in enumerate(refs[2 * terms :]):
        part = out.shape[1]
        for row, value in enumerate(values):
            out[row * tokens : (row + 1) * tokens] = value[:, index * part : (index + 1) * part].astype(BF)


def weight_grad_kernel(pieces, x_keep, x_recv, dy_keep, dy_recv, *refs):
    tokens = refs[0].shape[0] // 3
    x = jnp.concatenate([x_keep[...], x_recv[...]], axis=0)
    dy = jnp.concatenate([dy_keep[...], dy_recv[...]], axis=0)
    for index, ref in enumerate(refs[pieces:]):
        at = slice(index * tokens, (index + 1) * tokens)
        left = jnp.concatenate([piece[at] for piece in refs[:pieces]], axis=0)
        ref[...] = dot_rows(left, dy if index == 0 else x).astype(BF)


def shared_dx_kernel(blocks, halves, flag_ref, *refs):
    pieces = [refs[i * blocks : (i + 1) * blocks] for i in range(halves)]
    own_ref, oth_ref, *outs = refs[halves * blocks :]
    tokens = outs[0].shape[0]
    hidden, width = own_ref.shape[0] // 3, own_ref.shape[1]

    def collect(index):
        at = slice(index * tokens, (index + 1) * tokens)
        parts = [jnp.concatenate([ref[at] for ref in part], axis=0) for part in pieces]
        return jnp.concatenate(parts, axis=1)

    da, db = collect(1), collect(2)
    core = flag_ref[CORE]
    for place, ref in ((core, own_ref), (1 - core, oth_ref)):
        at = pl.ds(pl.multiple_of(place * width, 128), width)
        got = (dot(da, ref[:hidden]) + dot(db, ref[hidden : 2 * hidden])).astype(BF)
        parts = [got[j * tokens : (j + 1) * tokens] for j in range(blocks)]
        for j in range(blocks):
            outs[j][:, at] = parts[j]
        if len(outs) > blocks:
            outs[blocks][:, at] = jnp.where(flag_ref[ALIGNED] == 1, parts[1], parts[0])


def routed_kernel(pair, slices, waits, flag_ref, x_ref, dy_ref, gate_ref, up_ref, down_ref, *refs):
    new_gate, new_up, new_down, *refs = refs[waits:]
    outs, (acc, gate_acc, rows_x, rows_dy) = refs[:-4], refs[-4:]
    step = pl.program_id(0)
    slots, width = acc.shape
    piece = width // slices
    here = pl.ds(pl.multiple_of(flag_ref[LOCAL] * piece, 128), piece)
    there = pl.ds(pl.multiple_of((slices - 1 - flag_ref[LOCAL]) * piece, 128), piece)

    @pl.when(step == 0)
    def _():
        if pair:
            rows_x[:, here] = x_ref[:, :piece]
            rows_dy[:, here] = x_ref[:, piece:]
            rows_x[:, there] = dy_ref[:, :piece]
            rows_dy[:, there] = dy_ref[:, piece:]
        else:
            rows_x[...] = x_ref[...]
            rows_dy[...] = dy_ref[...]

    x = rows_x[...]
    dy = rows_dy[...]
    w_gate, w_up, w_down = gate_ref[0], up_ref[0], down_ref[0]
    pre_a = dot_cols(x, w_gate)
    pre_b = dot_cols(x, w_up)
    back_e = dot_cols(dy, w_down)
    sigm = jax.nn.sigmoid(pre_a)
    silu = pre_a * sigm
    hidden = silu * pre_b
    part = jnp.sum(back_e * hidden, axis=1, keepdims=True)
    grad_a = (back_e * pre_b * sigm * (1.0 + pre_a * (1.0 - sigm))).astype(BF)
    grad_b = (back_e * silu).astype(BF)
    row = dot(grad_a, w_gate) + dot(grad_b, w_up)
    new_gate[0] = dot_rows(grad_a, x).astype(BF)
    new_up[0] = dot_rows(grad_b, x).astype(BF)
    new_down[0] = dot_rows(hidden.astype(BF), dy).astype(BF)

    @pl.when(step == 0)
    def _():
        acc[...] = row
        gate_acc[...] = part

    @pl.when(step > 0)
    def _():
        acc[...] += row
        gate_acc[...] += part

    @pl.when(step == pl.num_programs(0) - 1)
    def _():
        lane = lax.broadcasted_iota(jnp.int32, (slots, 128), 1)
        sub = lax.broadcasted_iota(jnp.int32, (slots, 128), 0) % BLOCK
        spread = jnp.where(lane == sub, gate_acc[...], 0.0).reshape(slots // BLOCK, BLOCK, 128)
        line = jnp.sum(spread, axis=1, keepdims=True)
        line = jnp.broadcast_to(line, spread.shape).reshape(slots, 128)
        line = jnp.where(sub == GATE_ROW, line, 0.0)
        for index in range(slices):
            start = index * piece
            acc[:, start : start + 128] += line
        if pair:
            outs[0][...] = acc[:, here].astype(BF)
            outs[1][...] = acc[:, there].astype(BF)
        else:
            outs[0][...] = acc[...].astype(BF)


def combine_kernel(n_dp, flag_ref, expert_ref, slot_ref, gate_ref, rows_ref, *refs):
    dx_ref, gates_ref = refs[-2:]
    choices, tokens = slot_ref.shape
    slots = rows_ref.shape[0]
    line = lax.broadcasted_iota(jnp.int32, (slots, tokens), 0)
    sub = lax.broadcasted_iota(jnp.int32, (128, tokens), 0)
    pos = positions(expert_ref[...], slot_ref[...], n_dp)
    gate = gate_ref[...].astype(F32)
    rows = rows_ref[...]
    sel = jnp.zeros((slots, tokens), F32)
    for k in range(choices):
        at = pos[k : k + 1]
        sel = jnp.where(at == line, 1.0, sel)
        slot = at & (BLOCK - 1)
        pick = jnp.where((at >= 0) & (line == at - slot + GATE_ROW), 1.0, 0.0).astype(BF)
        found = dot_rows(rows[:, :128], pick)
        value = jnp.sum(jnp.where(sub == slot, found, 0.0), axis=0, keepdims=True)
        gates_ref[k : k + 1] = value / gate[k : k + 1]
    total = dot_rows(sel.astype(BF), rows)
    terms = refs[:-2]
    if len(terms) == 3:
        second = jnp.where(flag_ref[ALIGNED] == 1, terms[1][...], terms[2][...])
        total = total + terms[0][...].astype(F32) + second.astype(F32)
    else:
        total = total + terms[0][...].astype(F32)
    dx_ref[...] = total.astype(BF)


def add_kernel(own_ref, came_ref, out_ref):
    out_ref[...] = (own_ref[...].astype(F32) + came_ref[...].astype(F32)).astype(BF)


def total_kernel(flag_ref, own_ref, came_ref, next_ref, out_ref, pay_ref):
    total = (own_ref[...].astype(F32) + came_ref[...].astype(F32)).astype(BF)
    out_ref[...] = total
    pay_ref[...] = jnp.where(flag_ref[MIDDLE] == 1, total, next_ref[...])


def line_sum(value, n_node, depth):
    half = n_node // 2
    if n_node % 2:
        return lax.psum(value, "node")
    for k in range(half - 1):
        pairs = [(k, k + 1), (n_node - 1 - k, n_node - 2 - k)]
        got = lax.ppermute(value, "node", pairs)
        value = (value.astype(F32) + got.astype(F32)).astype(BF)
    got = lax.ppermute(value, "node", [(half - 1, half), (half, half - 1)])
    value = (value.astype(F32) + got.astype(F32)).astype(BF)
    for k in reversed(range(half - 1)):
        pairs = [(k + 1, k), (n_node - 2 - k, n_node - 1 - k)]
        got = lax.ppermute(value, "node", pairs)
        value = jnp.where(depth == k, got, value)
    return value


INWARD, CENTRE, OUTWARD = [(0, 1), (3, 2)], [(1, 2), (2, 1)], [(1, 0), (2, 3)]


class LineOfFour:
    def __init__(self, flags):
        self.flags = flags
        self.values, self.outer, self.sums, self.across, self.totals, self.ends = [], [], [], [], [], []
        self.last = []

    def add(self, values):
        self.values += values
        for value in self.values[len(self.outer) : 2]:
            self.outer.append(lax.ppermute(value, "node", INWARD))

    def step(self, kernel, name, operands, outs, after=(), held=(), flags=()):
        like = [shape(operands[0].shape, BF)] * outs
        got = call(kernel, like, operands, name, flags, self.last + list(after), held, LINE_BYTES)
        self.last = got[:1]
        return got

    def sum(self, after=()):
        now = len(self.sums)
        ahead = self.values[2:3] if now == 0 else []
        got = self.step(add_kernel, "line_sum", [self.values[now], self.outer[now]], 1, after, ahead)
        if ahead:
            self.values[2] = got[1]
            self.outer.append(lax.ppermute(got[1], "node", INWARD))
        self.sums.append(got[0])
        self.across.append(lax.ppermute(got[0], "node", CENTRE))

    def total(self, after=(), held=()):
        back = len(self.totals)
        operands = [self.sums[back], self.across[back]]
        waits = list(after) + (self.ends[back - 2 : back - 1] if back > 1 else [])
        if back + 3 < len(self.values):
            operands.append(self.values[back + 3])
            got = self.step(total_kernel, "line_total", operands, 2, waits, held, [self.flags])
            came = lax.ppermute(got[1], "node", INWARD + OUTWARD)
            self.outer.append(came)
            held = got[2:]
        else:
            got = self.step(add_kernel, "line_total", operands, 1, waits, held)
            came = lax.ppermute(got[0], "node", OUTWARD)
            held = got[1:]
        self.totals.append(got[0])
        self.ends.append(came)
        return list(held)

    def finish(self, middle):
        while len(self.sums) < len(self.values):
            self.sum()
        while len(self.totals) < len(self.values):
            self.total()
        return [jnp.where(middle, a, b) for a, b in zip(self.totals, self.ends)]


def on_device(
    layer_input,
    grad_out,
    gate_values,
    route_expert,
    route_slot,
    shared_gate,
    shared_up,
    shared_down,
    expert_gate,
    expert_up,
    expert_down,
):
    n_node = lax.axis_size("node")
    n_local = lax.axis_size("local")
    n_dp = lax.axis_size("dp")
    outer = n_dp // 2
    groups = n_node * n_dp
    slots = groups * BLOCK
    tokens, feat = layer_input.shape
    hidden_s, width = shared_gate.shape
    hidden_r, model = expert_gate.shape[1:]
    local = lax.axis_index("local")
    dp = lax.axis_index("dp")
    node = lax.axis_index("node")
    row, core = dp // 2, dp % 2
    paired = n_local == 2 and outer == 2
    middle = (node == 1) | (node == 2)
    flags = jnp.stack([core, row == local, local, middle]).astype(jnp.int32)

    swap_core = [(d, d ^ 1) for d in range(n_dp)]

    def outer_shift(step):
        return [(d, (d + 2 * step) % n_dp) for d in range(n_dp)]

    def at(l, y, c):
        return l * n_dp + 2 * y + c

    straight, diagonal = [], []
    if paired:
        for l in range(2):
            for c in range(2):
                straight.append((at(l, l, c), at(1 - l, l, c)))
                straight.append((at(l, 1 - l, c), at(l, l, c)))
                diagonal.append((at(l, 1 - l, c), at(1 - l, l, c)))
    backwards = [(b, a) for a, b in straight]

    def core_swap(value):
        return lax.ppermute(value, "dp", swap_core)

    def feature_blocks(own):
        if paired:
            first = lax.ppermute(own, ("local", "dp"), straight)
            second = lax.ppermute(own, ("local", "dp"), diagonal)
            return [own, first, second]
        full = lax.all_gather(own, "local", axis=1, tiled=True)
        found = [lax.dynamic_slice_in_dim(full, row * 2 * width, 2 * width, axis=1)]
        for step in range(1, outer):
            there = (row + outer - step) % outer
            piece = lax.dynamic_slice_in_dim(full, there * 2 * width, 2 * width, axis=1)
            found.append(lax.ppermute(piece, "dp", outer_shift(outer - step)))
        return found

    def gather_groups(value):
        near = [value]
        for step in range(1, outer):
            near.append(lax.ppermute(value, "dp", outer_shift(outer - step)))
        return near + [core_swap(v) for v in near]

    gate_values, route_expert, route_slot = gate_values.T, route_expert.T, route_slot.T
    x_blocks = feature_blocks(layer_input)
    dy_blocks = feature_blocks(grad_out)
    weights = [shared_gate, shared_up, shared_down]
    (shared,) = call(pack_kernel, [shape((3 * hidden_s, width), BF)], [far(v) for v in weights], "pack_weights")
    shared_oth = core_swap(shared)


    halves = 2 if hidden_s % 256 == 0 else 1
    part = hidden_s // halves

    def partial(blocks, weight, oth, first, mats, name, after):
        x_keep, x_send, *got = call(
            functools.partial(product_kernel, len(blocks), outer, first, mats),
            [shape((outer * tokens, width), BF)] * 2
            + [shape((mats * tokens, hidden_s), F32)]
            + [shape((mats * tokens, hidden_s), BF)] * (outer - 1),
            ([far(blocks[0])] + blocks[1:] if paired else blocks) + [weight, oth],
            name,
            [flags],
            after,
            far_outs=(0, 1, 2),
        )
        sums = [got[0]]
        for step in range(1, outer):
            sums.append(lax.ppermute(got[step], "dp", outer_shift(step)))
        return x_keep, core_swap(x_send), sums

    x_keep, x_recv, ab_sums = partial(x_blocks, shared, shared_oth, 0, 2, "shared_ab", [])
    (send_rows,) = call(
        functools.partial(select_kernel, n_dp),
        [shape((slots, 2 * feat), BF)],
        [far(v) for v in (route_expert, route_slot, gate_values, layer_input, grad_out)],
        "select_rows",
        after=ab_sums[1:2],
        far_outs=(0,),
    )
    back_rows = lax.all_to_all(
        send_rows.reshape(groups, BLOCK, 2 * feat),
        ("node", "dp"),
        split_axis=0,
        concat_axis=0,
        tiled=True,
    ).reshape(slots, 2 * feat)
    dy_keep, dy_recv, e_sums = partial(
        dy_blocks, shared, shared_oth, 2, 1, "shared_e", [far(ab_sums[0])]
    )
    values = call(
        functools.partial(slope_kernel, len(e_sums)),
        [shape((3 * tokens, part), BF)] * halves,
        [far(v) if v.dtype == F32 else v for v in ab_sums + e_sums],
        "shared_slopes",
        after=[x_recv, dy_recv, far(send_rows)],
    )
    pair = n_local == 2
    swap_local = [(0, 1), (1, 0)]
    if pair:
        row_operands = [back_rows, lax.ppermute(back_rows, "local", swap_local)]
    else:
        row_operands = [
            lax.all_gather(back_rows[:, :feat], "local", axis=1, tiled=True),
            lax.all_gather(back_rows[:, feat:], "local", axis=1, tiled=True),
        ]

    def weight_grads(pieces, after):
        rows = [x_keep, x_recv, dy_keep, dy_recv]
        return call(
            functools.partial(weight_grad_kernel, len(pieces)),
            [shape((part, width), BF)] * 3,
            [far(v) for v in rows] + pieces,
            "shared_weight_grads",
            after=after,
        )

    line = LineOfFour(flags) if n_node == 4 else None
    slopes = [gather_groups(values[0])]
    parts = weight_grads(slopes[0], ())
    if line:
        line.add(parts)
        parts = line.values

    row_outs = [shape((slots, feat), BF)] * 2 if pair else [shape((slots, model), BF)]
    waits = parts[:1]
    block = hidden_r // 2 if hidden_r % 128 == 0 else hidden_r
    tile = pl.BlockSpec((1, block, model), lambda i: (0, i, 0))
    experts = [far(v)[1] for v in (expert_gate, expert_up, expert_down)]
    new_gate, new_up, new_down, *rows_out = pl.pallas_call(
        functools.partial(routed_kernel, pair, n_local, len(waits)),
        grid=(hidden_r // block,),
        out_shape=[pltpu.HBM((1, hidden_r, model), BF)] * 3 + row_outs,
        in_specs=[SMEM]
        + [VMEM] * len(row_operands)
        + [tile, tile, tile]
        + [ANY] * len(waits),
        out_specs=[tile, tile, tile] + [VMEM] * len(row_outs),
        scratch_shapes=[
            pltpu.VMEM((slots, model), F32),
            pltpu.VMEM((slots, 1), F32),
            pltpu.VMEM((slots, model), BF),
            pltpu.VMEM((slots, model), BF),
        ],
        compiler_params=pltpu.CompilerParams(vmem_limit_bytes=24 * 1024 * 1024),
        cost_estimate=pl.CostEstimate(flops=0, bytes_accessed=0, transcendentals=0),
        name="routed_expert",
    )(flags, *row_operands, *experts, *waits)
    if pair:
        mine, gone = rows_out
        came = lax.ppermute(gone, "local", swap_local)
        row_sum = (mine.astype(F32) + came.astype(F32)).astype(BF)
    else:
        row_sum = lax.psum_scatter(rows_out[0], "local", scatter_dimension=1, tiled=True)
    for value in values[1:]:
        (value,) = call(lambda: None, [], [], "hold", after=slopes[-1][1:outer], held=[value])
        slopes.append(gather_groups(value))
        more = weight_grads(slopes[-1], rows_out[:1])
        if line:
            line.add(more)
        else:
            parts = parts + more
    if line:
        line.sum()
        line.sum(rows_out[:1])
        line.total()
    dx_blocks = call(
        functools.partial(shared_dx_kernel, outer, halves),
        [shape((tokens, 2 * width), BF)] * (outer + (1 if paired else 0)),
        sum((pieces[:outer] for pieces in slopes), []) + [shared, shared_oth],
        "shared_dx",
        [flags],
        line.last if line else (),
    )
    if line:
        line.sum(dx_blocks[:1])
        dx_blocks = line.total(held=dx_blocks)
        line.sum()
        line.total()
        line.sum()
        (row_sum,) = line.total(held=[row_sum])
    home = lax.all_to_all(
        row_sum.reshape(groups, BLOCK, feat),
        ("node", "dp"),
        split_axis=0,
        concat_axis=0,
        tiled=True,
    ).reshape(slots, feat)
    if line:
        line.sum()
        line.total()
    if paired:
        mine, other, straight_pay = dx_blocks
        first = lax.ppermute(straight_pay, ("local", "dp"), backwards)
        second = lax.ppermute(other, ("local", "dp"), diagonal)
        dx_terms = [first, mine, second]
    else:
        full = jnp.zeros((tokens, model), BF)
        for step, piece in enumerate(dx_blocks):
            if step:
                piece = lax.ppermute(piece, "dp", outer_shift(step))
            there = (row + outer - step) % outer
            full = lax.dynamic_update_slice_in_dim(full, piece, there * 2 * width, axis=1)
        dx_terms = [lax.psum_scatter(full, "local", scatter_dimension=1, tiled=True)]
    grad_x, grad_gates = call(
        functools.partial(combine_kernel, n_dp),
        [shape((tokens, feat), BF), shape(route_slot.shape, F32)],
        [far(v) for v in [route_expert, route_slot, gate_values, home] + dx_terms],
        "combine",
        [flags],
        line.last if line else (),
        far_outs=(0, 1),
    )
    if line:
        line.total([far(grad_gates)])
        parts = line.finish(middle)
    else:
        depth = jnp.minimum(node, n_node - 1 - node)
        parts = [line_sum(value, n_node, depth) for value in parts]
    grad_down, grad_gate, grad_up = (
        jnp.concatenate(parts[i::3], axis=0) if halves > 1 else parts[i] for i in range(3)
    )
    if n_local > 2:
        grad_gates = lax.psum(jnp.where(local == 0, grad_gates, 0.0), "local")
    return grad_x, grad_gates.T, grad_gate, grad_up, grad_down, new_gate, new_up, new_down


def solution(mesh):
    tokens = P(("node", "dp"), "local")
    choices = P(("node", "dp"), None)
    shared = P("local", "dp")
    expert = P(("node", "dp"), "local", None)
    return jax.shard_map(
        on_device,
        mesh=mesh,
        in_specs=(tokens, tokens, choices, choices, choices) + (shared,) * 3 + (expert,) * 3,
        out_specs=(tokens, choices) + (shared,) * 3 + (expert,) * 3,
        check_vma=False,
    )
```

```python
import functools

import jax
import jax.numpy as jnp
from jax import lax
from jax.experimental import pallas as pl
from jax.experimental.pallas import tpu as pltpu
from jax.sharding import PartitionSpec as P

NODE_EXPERTS = 10
BLOCK = 8
GATE_ROW = 6
CORE, ALIGNED, LOCAL, MIDDLE = range(4)
VMEM_BYTES = 16 * 1024 * 1024
LINE_BYTES = 8 * 1024 * 1024
BF = jnp.bfloat16
F32 = jnp.float32

SMEM = pl.BlockSpec(memory_space=pltpu.SMEM)
VMEM = pl.BlockSpec(memory_space=pltpu.VMEM)
ANY = pl.BlockSpec(memory_space=pl.ANY)


def dot_rows(left, right):
    return lax.dot_general(left, right, (((0,), (0,)), ((), ())), preferred_element_type=F32)


def dot_cols(left, right):
    return lax.dot_general(left, right, (((1,), (1,)), ((), ())), preferred_element_type=F32)


def dot(left, right):
    return lax.dot_general(left, right, (((1,), (0,)), ((), ())), preferred_element_type=F32)


def whole(dims):
    zeros = (0,) * len(dims)
    return pl.BlockSpec(dims, lambda i: zeros)


def far(value):
    return ("far", pltpu.with_memory_space_constraint(value, pltpu.HBM))


def call(kernel, outs, operands, name, flags=(), after=(), held=(), vmem=VMEM_BYTES, far_outs=()):
    count = len(flags) + len(operands)
    first = count + len(after)

    def body(*refs):
        kernel(*refs[:count], *refs[first + len(held) : len(refs) - len(held)])

    specs = [whole(v[1].shape) if isinstance(v, tuple) else VMEM for v in operands]
    operands = [v[1] if isinstance(v, tuple) else v for v in operands]
    after = [v[1] if isinstance(v, tuple) else v for v in after]
    got = pl.pallas_call(
        body,
        grid=(1,),
        out_shape=[pltpu.HBM(v.shape, v.dtype) if i in far_outs else v for i, v in enumerate(outs)]
        + [shape(v.shape, v.dtype) for v in held],
        in_specs=[SMEM] * len(flags) + specs + [ANY] * (len(after) + len(held)),
        out_specs=[whole(v.shape) if i in far_outs else VMEM for i, v in enumerate(outs)]
        + [ANY] * len(held),
        input_output_aliases={first + i: len(outs) + i for i in range(len(held))},
        compiler_params=pltpu.CompilerParams(vmem_limit_bytes=vmem),
        cost_estimate=pl.CostEstimate(flops=0, bytes_accessed=0, transcendentals=0),
        name=name,
    )(*flags, *operands, *after, *held)
    return list(got)


def shape(dims, dtype):
    return jax.ShapeDtypeStruct(dims, dtype)


def positions(expert, slot, n_dp):
    node = (expert * 205) >> 11
    held = node * n_dp + expert - node * NODE_EXPERTS
    return jnp.where(slot >= 0, held * BLOCK + slot, -1)


def pack_kernel(*refs):
    rows = refs[0].shape[0]
    for index, ref in enumerate(refs[:-1]):
        refs[-1][index * rows : (index + 1) * rows] = ref[...]


def select_kernel(n_dp, expert_ref, slot_ref, gate_ref, x_ref, dy_ref, out_ref):
    choices, tokens = slot_ref.shape
    slots = out_ref.shape[0]
    width = x_ref.shape[1]
    line = lax.broadcasted_iota(jnp.int32, (slots, tokens), 0)
    pos = positions(expert_ref[...], slot_ref[...], n_dp)
    gate = gate_ref[...].astype(F32)
    sel = jnp.zeros((slots, tokens), F32)
    selq = jnp.zeros((slots, tokens), F32)
    for k in range(choices):
        hit = pos[k : k + 1] == line
        sel = jnp.where(hit, 1.0, sel)
        selq = jnp.where(hit, gate[k : k + 1], selq)
    out_ref[:, :width] = dot(sel.astype(BF), x_ref[...]).astype(BF)
    out_ref[:, width:] = dot(selq.astype(BF), dy_ref[...]).astype(BF)


def product_kernel(inputs, blocks, first, mats, flag_ref, *refs):
    source = refs[:inputs]
    own_ref, oth_ref, keep_ref, send_ref, mine_ref, *away = refs[inputs:]
    tokens, width = source[0].shape[0], keep_ref.shape[1]
    hidden = mine_ref.shape[1]
    core = flag_ref[CORE]
    for place, out in ((core, keep_ref), (1 - core, send_ref)):
        at = pl.ds(pl.multiple_of(place * width, 128), width)
        parts = [ref[:, at] for ref in source]
        if inputs > blocks:
            aligned = flag_ref[ALIGNED] == 1
            parts = [jnp.where(aligned, parts[0], parts[1]), jnp.where(aligned, parts[1], parts[2])]
        for j, part in enumerate(parts):
            out[j * tokens : (j + 1) * tokens] = part
    keep, send = keep_ref[...], send_ref[...]
    for index in range(mats):
        weight = slice((first + index) * hidden, (first + index + 1) * hidden)
        product = dot_cols(keep, own_ref[weight]) + dot_cols(send, oth_ref[weight])
        at = slice(index * tokens, (index + 1) * tokens)
        mine_ref[at] = product[:tokens]
        for j, ref in enumerate(away):
            ref[at] = product[(j + 1) * tokens : (j + 2) * tokens].astype(BF)


def slope_kernel(terms, *refs):
    def total(part):
        value = part[0][...]
        for ref in part[1:]:
            value = value + ref[...].astype(F32)
        return value

    both, e = total(refs[:terms]), total(refs[terms : 2 * terms])
    tokens = e.shape[0]
    a, b = both[:tokens], both[tokens:]
    sigm = jax.nn.sigmoid(a)
    silu = a * sigm
    values = (silu * b, e * b * sigm * (1.0 + a * (1.0 - sigm)), e * silu)
    for index, out in enumerate(refs[2 * terms :]):
        part = out.shape[1]
        for row, value in enumerate(values):
            out[row * tokens : (row + 1) * tokens] = value[:, index * part : (index + 1) * part].astype(BF)


def weight_grad_kernel(pieces, x_keep, x_recv, dy_keep, dy_recv, *refs):
    tokens = refs[0].shape[0] // 3
    x = jnp.concatenate([x_keep[...], x_recv[...]], axis=0)
    dy = jnp.concatenate([dy_keep[...], dy_recv[...]], axis=0)
    for index, ref in enumerate(refs[pieces:]):
        at = slice(index * tokens, (index + 1) * tokens)
        left = jnp.concatenate([piece[at] for piece in refs[:pieces]], axis=0)
        ref[...] = dot_rows(left, dy if index == 0 else x).astype(BF)


def shared_dx_kernel(blocks, halves, flag_ref, *refs):
    pieces = [refs[i * blocks : (i + 1) * blocks] for i in range(halves)]
    own_ref, oth_ref, *outs = refs[halves * blocks :]
    tokens = outs[0].shape[0]
    hidden, width = own_ref.shape[0] // 3, own_ref.shape[1]

    def collect(index):
        at = slice(index * tokens, (index + 1) * tokens)
        parts = [jnp.concatenate([ref[at] for ref in part], axis=0) for part in pieces]
        return jnp.concatenate(parts, axis=1)

    da, db = collect(1), collect(2)
    core = flag_ref[CORE]
    for place, ref in ((core, own_ref), (1 - core, oth_ref)):
        at = pl.ds(pl.multiple_of(place * width, 128), width)
        got = (dot(da, ref[:hidden]) + dot(db, ref[hidden : 2 * hidden])).astype(BF)
        parts = [got[j * tokens : (j + 1) * tokens] for j in range(blocks)]
        for j in range(blocks):
            outs[j][:, at] = parts[j]
        if len(outs) > blocks:
            outs[blocks][:, at] = jnp.where(flag_ref[ALIGNED] == 1, parts[1], parts[0])


def routed_kernel(pair, slices, waits, flag_ref, x_ref, dy_ref, gate_ref, up_ref, down_ref, *refs):
    new_gate, new_up, new_down, *refs = refs[waits:]
    outs, (acc, gate_acc, rows_x, rows_dy) = refs[:-4], refs[-4:]
    step = pl.program_id(0)
    slots, width = acc.shape
    piece = width // slices
    here = pl.ds(pl.multiple_of(flag_ref[LOCAL] * piece, 128), piece)
    there = pl.ds(pl.multiple_of((slices - 1 - flag_ref[LOCAL]) * piece, 128), piece)

    @pl.when(step == 0)
    def _():
        if pair:
            rows_x[:, here] = x_ref[:, :piece]
            rows_dy[:, here] = x_ref[:, piece:]
            rows_x[:, there] = dy_ref[:, :piece]
            rows_dy[:, there] = dy_ref[:, piece:]
        else:
            rows_x[...] = x_ref[...]
            rows_dy[...] = dy_ref[...]

    x = rows_x[...]
    dy = rows_dy[...]
    w_gate, w_up, w_down = gate_ref[0], up_ref[0], down_ref[0]
    pre_a = dot_cols(x, w_gate)
    pre_b = dot_cols(x, w_up)
    back_e = dot_cols(dy, w_down)
    sigm = jax.nn.sigmoid(pre_a)
    silu = pre_a * sigm
    hidden = silu * pre_b
    part = jnp.sum(back_e * hidden, axis=1, keepdims=True)
    grad_a = (back_e * pre_b * sigm * (1.0 + pre_a * (1.0 - sigm))).astype(BF)
    grad_b = (back_e * silu).astype(BF)
    row = dot(grad_a, w_gate) + dot(grad_b, w_up)
    new_gate[0] = dot_rows(grad_a, x).astype(BF)
    new_up[0] = dot_rows(grad_b, x).astype(BF)
    new_down[0] = dot_rows(hidden.astype(BF), dy).astype(BF)

    @pl.when(step == 0)
    def _():
        acc[...] = row
        gate_acc[...] = part

    @pl.when(step > 0)
    def _():
        acc[...] += row
        gate_acc[...] += part

    @pl.when(step == pl.num_programs(0) - 1)
    def _():
        lane = lax.broadcasted_iota(jnp.int32, (slots, 128), 1)
        sub = lax.broadcasted_iota(jnp.int32, (slots, 128), 0) % BLOCK
        spread = jnp.where(lane == sub, gate_acc[...], 0.0).reshape(slots // BLOCK, BLOCK, 128)
        line = jnp.sum(spread, axis=1, keepdims=True)
        line = jnp.broadcast_to(line, spread.shape).reshape(slots, 128)
        line = jnp.where(sub == GATE_ROW, line, 0.0)
        for index in range(slices):
            start = index * piece
            acc[:, start : start + 128] += line
        if pair:
            outs[0][...] = acc[:, here].astype(BF)
            outs[1][...] = acc[:, there].astype(BF)
        else:
            outs[0][...] = acc[...].astype(BF)


def combine_kernel(n_dp, flag_ref, expert_ref, slot_ref, gate_ref, rows_ref, *refs):
    dx_ref, gates_ref = refs[-2:]
    choices, tokens = slot_ref.shape
    slots = rows_ref.shape[0]
    line = lax.broadcasted_iota(jnp.int32, (slots, tokens), 0)
    sub = lax.broadcasted_iota(jnp.int32, (128, tokens), 0)
    pos = positions(expert_ref[...], slot_ref[...], n_dp)
    gate = gate_ref[...].astype(F32)
    rows = rows_ref[...]
    sel = jnp.zeros((slots, tokens), F32)
    for k in range(choices):
        at = pos[k : k + 1]
        sel = jnp.where(at == line, 1.0, sel)
        slot = at & (BLOCK - 1)
        pick = jnp.where((at >= 0) & (line == at - slot + GATE_ROW), 1.0, 0.0).astype(BF)
        found = dot_rows(rows[:, :128], pick)
        value = jnp.sum(jnp.where(sub == slot, found, 0.0), axis=0, keepdims=True)
        gates_ref[k : k + 1] = value / gate[k : k + 1]
    total = dot_rows(sel.astype(BF), rows)
    terms = refs[:-2]
    if len(terms) == 3:
        second = jnp.where(flag_ref[ALIGNED] == 1, terms[1][...], terms[2][...])
        total = total + terms[0][...].astype(F32) + second.astype(F32)
    else:
        total = total + terms[0][...].astype(F32)
    dx_ref[...] = total.astype(BF)


def add_kernel(own_ref, came_ref, out_ref):
    out_ref[...] = (own_ref[...].astype(F32) + came_ref[...].astype(F32)).astype(BF)


def total_kernel(flag_ref, own_ref, came_ref, next_ref, out_ref, pay_ref):
    total = (own_ref[...].astype(F32) + came_ref[...].astype(F32)).astype(BF)
    out_ref[...] = total
    pay_ref[...] = jnp.where(flag_ref[MIDDLE] == 1, total, next_ref[...])


def line_sum(value, n_node, depth):
    half = n_node // 2
    if n_node % 2:
        return lax.psum(value, "node")
    for k in range(half - 1):
        pairs = [(k, k + 1), (n_node - 1 - k, n_node - 2 - k)]
        got = lax.ppermute(value, "node", pairs)
        value = (value.astype(F32) + got.astype(F32)).astype(BF)
    got = lax.ppermute(value, "node", [(half - 1, half), (half, half - 1)])
    value = (value.astype(F32) + got.astype(F32)).astype(BF)
    for k in reversed(range(half - 1)):
        pairs = [(k + 1, k), (n_node - 2 - k, n_node - 1 - k)]
        got = lax.ppermute(value, "node", pairs)
        value = jnp.where(depth == k, got, value)
    return value


INWARD, CENTRE, OUTWARD = [(0, 1), (3, 2)], [(1, 2), (2, 1)], [(1, 0), (2, 3)]


class LineOfFour:
    def __init__(self, flags):
        self.flags = flags
        self.values, self.outer, self.sums, self.across, self.totals, self.ends = [], [], [], [], [], []
        self.last = []

    def add(self, values):
        self.values += values
        for value in self.values[len(self.outer) : 2]:
            self.outer.append(lax.ppermute(value, "node", INWARD))

    def step(self, kernel, name, operands, outs, after=(), held=(), flags=()):
        like = [shape(operands[0].shape, BF)] * outs
        got = call(kernel, like, operands, name, flags, self.last + list(after), held, LINE_BYTES)
        self.last = got[:1]
        return got

    def sum(self, after=()):
        now = len(self.sums)
        ahead = self.values[2:3] if now == 0 else []
        got = self.step(add_kernel, "line_sum", [self.values[now], self.outer[now]], 1, after, ahead)
        if ahead:
            self.values[2] = got[1]
            self.outer.append(lax.ppermute(got[1], "node", INWARD))
        self.sums.append(got[0])
        self.across.append(lax.ppermute(got[0], "node", CENTRE))

    def total(self, after=(), held=()):
        back = len(self.totals)
        operands = [self.sums[back], self.across[back]]
        waits = list(after) + (self.ends[back - 2 : back - 1] if back > 1 else [])
        if back + 3 < len(self.values):
            operands.append(self.values[back + 3])
            got = self.step(total_kernel, "line_total", operands, 2, waits, held, [self.flags])
            came = lax.ppermute(got[1], "node", INWARD + OUTWARD)
            self.outer.append(came)
            held = got[2:]
        else:
            got = self.step(add_kernel, "line_total", operands, 1, waits, held)
            came = lax.ppermute(got[0], "node", OUTWARD)
            held = got[1:]
        self.totals.append(got[0])
        self.ends.append(came)
        return list(held)

    def finish(self, middle):
        while len(self.sums) < len(self.values):
            self.sum()
        while len(self.totals) < len(self.values):
            self.total()
        return [jnp.where(middle, a, b) for a, b in zip(self.totals, self.ends)]


def on_device(
    layer_input,
    grad_out,
    gate_values,
    route_expert,
    route_slot,
    shared_gate,
    shared_up,
    shared_down,
    expert_gate,
    expert_up,
    expert_down,
):
    n_node = lax.axis_size("node")
    n_local = lax.axis_size("local")
    n_dp = lax.axis_size("dp")
    outer = n_dp // 2
    groups = n_node * n_dp
    slots = groups * BLOCK
    tokens, feat = layer_input.shape
    hidden_s, width = shared_gate.shape
    hidden_r, model = expert_gate.shape[1:]
    local = lax.axis_index("local")
    dp = lax.axis_index("dp")
    node = lax.axis_index("node")
    row, core = dp // 2, dp % 2
    paired = n_local == 2 and outer == 2
    middle = (node == 1) | (node == 2)
    flags = jnp.stack([core, row == local, local, middle]).astype(jnp.int32)

    swap_core = [(d, d ^ 1) for d in range(n_dp)]

    def outer_shift(step):
        return [(d, (d + 2 * step) % n_dp) for d in range(n_dp)]

    def at(l, y, c):
        return l * n_dp + 2 * y + c

    straight, diagonal = [], []
    if paired:
        for l in range(2):
            for c in range(2):
                straight.append((at(l, l, c), at(1 - l, l, c)))
                straight.append((at(l, 1 - l, c), at(l, l, c)))
                diagonal.append((at(l, 1 - l, c), at(1 - l, l, c)))
    backwards = [(b, a) for a, b in straight]

    def core_swap(value):
        return lax.ppermute(value, "dp", swap_core)

    def feature_blocks(own):
        if paired:
            first = lax.ppermute(own, ("local", "dp"), straight)
            second = lax.ppermute(own, ("local", "dp"), diagonal)
            return [own, first, second]
        full = lax.all_gather(own, "local", axis=1, tiled=True)
        found = [lax.dynamic_slice_in_dim(full, row * 2 * width, 2 * width, axis=1)]
        for step in range(1, outer):
            there = (row + outer - step) % outer
            piece = lax.dynamic_slice_in_dim(full, there * 2 * width, 2 * width, axis=1)
            found.append(lax.ppermute(piece, "dp", outer_shift(outer - step)))
        return found

    def gather_groups(value):
        near = [value]
        for step in range(1, outer):
            near.append(lax.ppermute(value, "dp", outer_shift(outer - step)))
        return near + [core_swap(v) for v in near]

    gate_values, route_expert, route_slot = gate_values.T, route_expert.T, route_slot.T
    x_blocks = feature_blocks(layer_input)
    dy_blocks = feature_blocks(grad_out)
    weights = [shared_gate, shared_up, shared_down]
    (shared,) = call(pack_kernel, [shape((3 * hidden_s, width), BF)], [far(v) for v in weights], "pack_weights")
    shared_oth = core_swap(shared)


    halves = 2 if hidden_s % 256 == 0 else 1
    part = hidden_s // halves

    def partial(blocks, weight, oth, first, mats, name, after):
        x_keep, x_send, *got = call(
            functools.partial(product_kernel, len(blocks), outer, first, mats),
            [shape((outer * tokens, width), BF)] * 2
            + [shape((mats * tokens, hidden_s), F32)]
            + [shape((mats * tokens, hidden_s), BF)] * (outer - 1),
            ([far(blocks[0])] + blocks[1:] if paired else blocks) + [weight, oth],
            name,
            [flags],
            after,
            far_outs=(0, 1, 2),
        )
        sums = [got[0]]
        for step in range(1, outer):
            sums.append(lax.ppermute(got[step], "dp", outer_shift(step)))
        return x_keep, core_swap(x_send), sums

    (send_rows,) = call(
        functools.partial(select_kernel, n_dp),
        [shape((slots, 2 * feat), BF)],
        [far(v) for v in (route_expert, route_slot, gate_values, layer_input, grad_out)],
        "select_rows",
        after=[shared],
        far_outs=(0,),
    )
    back_rows = lax.all_to_all(
        send_rows.reshape(groups, BLOCK, 2 * feat),
        ("node", "dp"),
        split_axis=0,
        concat_axis=0,
        tiled=True,
    ).reshape(slots, 2 * feat)

    x_keep, x_recv, ab_sums = partial(x_blocks, shared, shared_oth, 0, 2, "shared_ab", [far(send_rows)])
    dy_keep, dy_recv, e_sums = partial(
        dy_blocks, shared, shared_oth, 2, 1, "shared_e", [far(ab_sums[0])]
    )
    values = call(
        functools.partial(slope_kernel, len(e_sums)),
        [shape((3 * tokens, part), BF)] * halves,
        [far(v) if v.dtype == F32 else v for v in ab_sums + e_sums],
        "shared_slopes",
        after=[x_recv, dy_recv],
    )
    pair = n_local == 2
    swap_local = [(0, 1), (1, 0)]
    if pair:
        row_operands = [back_rows, lax.ppermute(back_rows, "local", swap_local)]
    else:
        row_operands = [
            lax.all_gather(back_rows[:, :feat], "local", axis=1, tiled=True),
            lax.all_gather(back_rows[:, feat:], "local", axis=1, tiled=True),
        ]

    def weight_grads(pieces, after):
        rows = [x_keep, x_recv, dy_keep, dy_recv]
        return call(
            functools.partial(weight_grad_kernel, len(pieces)),
            [shape((part, width), BF)] * 3,
            [far(v) for v in rows] + pieces,
            "shared_weight_grads",
            after=after,
        )

    line = LineOfFour(flags) if n_node == 4 else None
    slopes = [gather_groups(values[0])]
    parts = weight_grads(slopes[0], ())
    if line:
        line.add(parts)
        parts = line.values

    for value in values[1:]:
        (value,) = call(lambda: None, [], [], "hold", after=slopes[-1][1:outer], held=[value])
        slopes.append(gather_groups(value))
        more = weight_grads(slopes[-1], ())
        if line:
            line.add(more)
        else:
            parts = parts + more
    if line:
        line.sum(parts[-1:])

    row_outs = [shape((slots, feat), BF)] * 2 if pair else [shape((slots, model), BF)]
    waits = parts[-1:] + (line.last if line else [])
    block = hidden_r // 2 if hidden_r % 128 == 0 else hidden_r
    tile = pl.BlockSpec((1, block, model), lambda i: (0, i, 0))
    experts = [far(v)[1] for v in (expert_gate, expert_up, expert_down)]
    new_gate, new_up, new_down, *rows_out = pl.pallas_call(
        functools.partial(routed_kernel, pair, n_local, len(waits)),
        grid=(hidden_r // block,),
        out_shape=[pltpu.HBM((1, hidden_r, model), BF)] * 3 + row_outs,
        in_specs=[SMEM]
        + [VMEM] * len(row_operands)
        + [tile, tile, tile]
        + [ANY] * len(waits),
        out_specs=[tile, tile, tile] + [VMEM] * len(row_outs),
        scratch_shapes=[
            pltpu.VMEM((slots, model), F32),
            pltpu.VMEM((slots, 1), F32),
            pltpu.VMEM((slots, model), BF),
            pltpu.VMEM((slots, model), BF),
        ],
        compiler_params=pltpu.CompilerParams(vmem_limit_bytes=24 * 1024 * 1024),
        cost_estimate=pl.CostEstimate(flops=0, bytes_accessed=0, transcendentals=0),
        name="routed_expert",
    )(flags, *row_operands, *experts, *waits)
    if pair:
        mine, gone = rows_out
        came = lax.ppermute(gone, "local", swap_local)
        row_sum = (mine.astype(F32) + came.astype(F32)).astype(BF)
    else:
        row_sum = lax.psum_scatter(rows_out[0], "local", scatter_dimension=1, tiled=True)
    if line:
        line.sum(rows_out[:1])
        line.total()
    dx_blocks = call(
        functools.partial(shared_dx_kernel, outer, halves),
        [shape((tokens, 2 * width), BF)] * (outer + (1 if paired else 0)),
        sum((pieces[:outer] for pieces in slopes), []) + [shared, shared_oth],
        "shared_dx",
        [flags],
        line.last if line else (),
    )
    if line:
        line.sum(dx_blocks[:1])
        dx_blocks = line.total(held=dx_blocks)
        line.sum()
        line.total()
        line.sum()
        (row_sum,) = line.total(held=[row_sum])
    home = lax.all_to_all(
        row_sum.reshape(groups, BLOCK, feat),
        ("node", "dp"),
        split_axis=0,
        concat_axis=0,
        tiled=True,
    ).reshape(slots, feat)
    if line:
        line.sum()
        line.total()
    if paired:
        mine, other, straight_pay = dx_blocks
        first = lax.ppermute(straight_pay, ("local", "dp"), backwards)
        second = lax.ppermute(other, ("local", "dp"), diagonal)
        dx_terms = [first, mine, second]
    else:
        full = jnp.zeros((tokens, model), BF)
        for step, piece in enumerate(dx_blocks):
            if step:
                piece = lax.ppermute(piece, "dp", outer_shift(step))
            there = (row + outer - step) % outer
            full = lax.dynamic_update_slice_in_dim(full, piece, there * 2 * width, axis=1)
        dx_terms = [lax.psum_scatter(full, "local", scatter_dimension=1, tiled=True)]
    grad_x, grad_gates = call(
        functools.partial(combine_kernel, n_dp),
        [shape((tokens, feat), BF), shape(route_slot.shape, F32)],
        [far(v) for v in [route_expert, route_slot, gate_values, home] + dx_terms],
        "combine",
        [flags],
        line.last if line else (),
        far_outs=(0, 1),
    )
    if line:
        line.total([far(grad_gates)])
        parts = line.finish(middle)
    else:
        depth = jnp.minimum(node, n_node - 1 - node)
        parts = [line_sum(value, n_node, depth) for value in parts]
    grad_down, grad_gate, grad_up = (
        jnp.concatenate(parts[i::3], axis=0) if halves > 1 else parts[i] for i in range(3)
    )
    if n_local > 2:
        grad_gates = lax.psum(jnp.where(local == 0, grad_gates, 0.0), "local")
    return grad_x, grad_gates.T, grad_gate, grad_up, grad_down, new_gate, new_up, new_down


def solution(mesh):
    tokens = P(("node", "dp"), "local")
    choices = P(("node", "dp"), None)
    shared = P("local", "dp")
    expert = P(("node", "dp"), "local", None)
    return jax.shard_map(
        on_device,
        mesh=mesh,
        in_specs=(tokens, tokens, choices, choices, choices) + (shared,) * 3 + (expert,) * 3,
        out_specs=(tokens, choices) + (shared,) * 3 + (expert,) * 3,
        check_vma=False,
    )
```
